32 devices in a mesh: groups: 2 (over y), seq: 4 (over z), tensor: 4 (over x, core).
Axes of the slice: x: 2, y: 2, z: 4, core: 2. Of those that a mesh axis runs over, the one named last changes fastest.
Arguments:
- text_states: bfloat16 [64, 8192], P(('groups', 'seq')), parts along dimension 0, may hold values from -18 to 18
- vision_states: bfloat16 [2048, 8192], P(('groups', 'seq'), 'tensor'), parts along dimension 0, may hold values from -6 to 6
- norm_gain: bfloat16 [8192], replicated, may hold values from 0.25 to 1.75
- query_weight: bfloat16 [8192, 8192], P('seq', 'tensor'), may hold values from -0.0625 to 0.0625
- key_value_weight: bfloat16 [2, 8192, 1024], P(None, 'tensor', 'seq'), may hold values from -0.0625 to 0.0625
- out_weight: bfloat16 [8192, 8192], P('tensor', 'seq'), may hold values from -0.0625 to 0.0625
- query_gain: float32 [128], replicated, may hold values from 4.5 to 6
- key_norm_gain: float32 [128], replicated, may hold values from 4.5 to 6
- attn_gate: float32 [1], replicated, may hold values from 0.4 to 2
- tile_counts: int32 [4], P('groups'), parts along dimension 0, may hold values from 128 to 512, as said below
- tile_mask: int32 [2, 2], P('groups'), parts along dimension 0, may hold values from 0 to 1, as said below
Outputs:
- layer_out: bfloat16 [64, 8192], P(('groups', 'tensor'), 'seq'), parts along dimension 0
The draws below stay inside these ranges and needn't reach their ends.
There are 2 independent parts, one for each index of `groups`. The reference program is written for one: setup_inputs(seed, part) draws one part's arguments, and reference() takes and returns one part's arrays. A program takes and returns all parts, laid end to end along the dimension named above; an argument that names none is the same for every part. Nothing has to cross between parts.
Inputs may be any that keep to these rules, and one draw needn't show every extreme that they name: `tile_counts`: some tile is full (512 valid tokens) and some tile holds exactly 128; valid tokens are the first slots of a tile. `tile_mask`: every row has at least one 1 and at least one 0.
All inputs are finite; a program needn't handle non-finite values.
Results may differ from the reference program's by a relative error of at most 0.0055.
The reference program's roundings to bfloat16 on the way count: a program that leaves them out, or rounds other values in their place, can miss the bound.
Values may be sent and summed in bfloat16 or wider, within the bound.
A program may use at most 128 MiB of HBM per device.

```python
import jax
import jax.numpy as jnp
from jax import lax

MODEL_WIDTH = 8192
QUERY_HEADS = 64
KEY_VALUE_HEADS = 8
HEAD_DIMENSION = 128
TILE_LEN = 512
TEXT_BLOCK = 32
TEXT_TOKENS = 32
VISION_SLOTS = 1024
TILES = 2
BLOCKS = 1


def draw_text_states(key, part):
    base = jax.random.truncated_normal(jax.random.fold_in(key, 1), -6.0, 6.0, (TEXT_TOKENS, MODEL_WIDTH), jnp.float32)
    return base.astype(jnp.bfloat16)


def gain_pair(key):
    base = jax.random.fold_in(key, 11)
    query_part = jax.random.uniform(jax.random.fold_in(base, 1), (HEAD_DIMENSION,), jnp.float32, 4.5, 6.0)
    key_part = jax.random.uniform(jax.random.fold_in(base, 2), (HEAD_DIMENSION,), jnp.float32, 4.5, 6.0)
    return (query_part, key_part)


def draw_query_gain(key, part):
    return gain_pair(key)[0].astype(jnp.float32)


def draw_key_norm_gain(key, part):
    return gain_pair(key)[1].astype(jnp.float32)


def draw_tile_counts(key, part):
    counts = jax.random.randint(jax.random.fold_in(key, 21), (TILES,), TILE_LEN // 4, TILE_LEN + 1)
    full = jax.random.randint(jax.random.fold_in(key, 22), (), 0, TILES)
    low = (full + 1 + jax.random.randint(jax.random.fold_in(key, 23), (), 0, TILES - 1)) % TILES
    places = jnp.arange(TILES)
    counts = jnp.where(places == full, TILE_LEN, counts)
    counts = jnp.where(places == low, TILE_LEN // 4, counts)
    return counts.astype(jnp.int32)


def draw_tile_mask(key, part):
    coins = jax.random.randint(jax.random.fold_in(key, 31), (BLOCKS, TILES), 0, 2)
    picked = jax.random.randint(jax.random.fold_in(key, 32), (BLOCKS,), 0, TILES)
    offset = jax.random.randint(jax.random.fold_in(key, 33), (BLOCKS,), 0, TILES - 1)
    zero_at = (picked + 1 + offset) % TILES
    places = jnp.arange(TILES)[None, :]
    forced = (places == picked[:, None]).astype(jnp.int32)
    mask = jnp.maximum(coins, forced)
    mask = jnp.where(places == zero_at[:, None], 0, mask)
    return mask.astype(jnp.int32)


def steps_of(stream_key, dims, cuts, smallest, largest):
    loudness, own = 1.0, jax.random.fold_in(stream_key, 6)
    for dim, parts in cuts:
        draws = jnp.exp(jax.random.uniform(jax.random.fold_in(own, dim), (parts,), jnp.float32, smallest / len(cuts), largest / len(cuts)))
        loudness = loudness * jnp.repeat(draws, dims[dim] // parts).reshape([-1 if axis == dim else 1 for axis in range(len(dims))])
    return loudness


def noise(key, dims, deviation, bound, shards=(), kind=jnp.bfloat16):
    loudness = steps_of(key, dims, shards, -0.22, 0.18) if shards else 1.0
    entries = jax.random.normal(key, dims, jnp.float32) * deviation * loudness
    return jnp.minimum(jnp.maximum(entries, -bound), bound).astype(kind)


def setup_inputs(seed: int = 0, part: int = 0) -> dict:
    key_list = jax.random.split(jax.random.key(seed), 12)
    part_keys = jax.random.split(jax.random.fold_in(key_list[11], part), 12)
    return {
        "text_states": draw_text_states(jax.random.fold_in(jax.random.fold_in(key_list[11], part), 71), part),
        "vision_states": noise(part_keys[1], (VISION_SLOTS, MODEL_WIDTH), 1.0, 6.0, ((0, 4), (1, 4))),
        "norm_gain": jnp.clip(1.0 + 0.15 * jax.random.normal(key_list[2], (MODEL_WIDTH,), jnp.float32), 0.25, 1.75).astype(jnp.bfloat16),
        "query_weight": noise(key_list[3], (MODEL_WIDTH, QUERY_HEADS * HEAD_DIMENSION), MODEL_WIDTH ** -0.5, 0.0625, ((0, 4), (1, 4))),
        "key_value_weight": noise(key_list[4], (2, MODEL_WIDTH, KEY_VALUE_HEADS * HEAD_DIMENSION), MODEL_WIDTH ** -0.5, 0.0625, ((1, 4), (2, 4))),
        "out_weight": noise(key_list[5], (QUERY_HEADS * HEAD_DIMENSION, MODEL_WIDTH), (QUERY_HEADS * HEAD_DIMENSION) ** -0.5, 0.0625, ((0, 4), (1, 4))),
        "query_gain": draw_query_gain(jax.random.fold_in(key_list[11], 71), part),
        "key_norm_gain": draw_key_norm_gain(jax.random.fold_in(key_list[11], 71), part),
        "attn_gate": jnp.clip(jax.random.uniform(key_list[8], (1,), jnp.float32, 0.4, 2.0), 0.4, 2.0),
        "tile_counts": draw_tile_counts(jax.random.fold_in(jax.random.fold_in(key_list[11], part), 71), part),
        "tile_mask": draw_tile_mask(jax.random.fold_in(jax.random.fold_in(key_list[11], part), 71), part),
    }


EPS = 1e-05
NEG = -1e+30

def root_mean_rows(value_matrix, gain):
    mean_sq = lax.optimization_barrier(jnp.mean(value_matrix * value_matrix, axis=-1, keepdims=True))
    return value_matrix * lax.rsqrt(mean_sq + EPS) * gain

def reference(text_states, vision_states, norm_gain, query_weight, key_value_weight, out_weight, query_gain, key_norm_gain, attn_gate, tile_counts, tile_mask):
    text_wide = text_states.astype(jnp.float32)
    normed = root_mean_rows(text_wide, norm_gain.astype(jnp.float32)).astype(jnp.bfloat16)
    query_raw = jnp.dot(normed, query_weight, preferred_element_type=jnp.float32)
    query_matrix = root_mean_rows(query_raw.reshape(TEXT_TOKENS, QUERY_HEADS, HEAD_DIMENSION), query_gain).astype(jnp.bfloat16)
    unnormed_keys = jnp.dot(vision_states, key_value_weight[0], preferred_element_type=jnp.float32)
    unnormed_values = jnp.dot(vision_states, key_value_weight[1], preferred_element_type=jnp.float32)
    key_matrix = root_mean_rows(unnormed_keys.reshape(VISION_SLOTS, KEY_VALUE_HEADS, HEAD_DIMENSION), key_norm_gain).astype(jnp.bfloat16)
    value_matrix = unnormed_values.astype(jnp.bfloat16).reshape(VISION_SLOTS, KEY_VALUE_HEADS, HEAD_DIMENSION)
    slot = jnp.arange(VISION_SLOTS, dtype=jnp.int32)
    slot_tile = slot // TILE_LEN
    slot_ok = slot % TILE_LEN < tile_counts[slot_tile]
    text_block = jnp.arange(TEXT_TOKENS, dtype=jnp.int32) // TEXT_BLOCK
    allowed = (tile_mask[text_block][:, slot_tile] == 1) & slot_ok[None, :]
    group_size = QUERY_HEADS // KEY_VALUE_HEADS
    scale = HEAD_DIMENSION ** (-0.5)
    heads_of_query = jnp.transpose(query_matrix.reshape(TEXT_TOKENS, KEY_VALUE_HEADS, group_size, HEAD_DIMENSION), (1, 0, 2, 3))
    key_heads = jnp.transpose(key_matrix, (1, 0, 2))
    value_heads = jnp.transpose(value_matrix, (1, 0, 2))

    def one_head(operands):
        query_part, key_part, value_part = operands
        scores = jnp.einsum('igd,vd->igv', query_part.astype(jnp.float32), key_part.astype(jnp.float32), precision=lax.Precision.HIGHEST) * scale
        mask = allowed[:, None, :]
        masked = jnp.where(mask, scores, NEG)
        top = lax.optimization_barrier(jnp.max(masked, axis=-1, keepdims=True))
        weights = jnp.where(mask, jnp.exp(masked - top), 0.0)
        total = lax.optimization_barrier(jnp.sum(weights, axis=-1, keepdims=True))
        summed = jnp.einsum('igv,vd->igd', weights, value_part.astype(jnp.float32), precision=lax.Precision.HIGHEST)
        return summed / total
    attended = lax.map(one_head, (heads_of_query, key_heads, value_heads))
    attention = jnp.transpose(attended, (1, 0, 2, 3)).reshape(TEXT_TOKENS, QUERY_HEADS * HEAD_DIMENSION).astype(jnp.bfloat16)
    branch = jnp.dot(attention, out_weight, preferred_element_type=jnp.float32)
    return (text_wide + jnp.tanh(attn_gate[0]) * branch).astype(jnp.bfloat16)
```

```python
import jax
import jax.numpy as jnp
from jax import lax
from jax.experimental import pallas as pl
from jax.experimental.pallas import tpu as pltpu
from jax.sharding import PartitionSpec as P

TILE_LEN = 512
TEXT_BLOCK = 32


EPS = 1e-05
NEG = -1e30


def combined_all(part, axis, combine):
    gathered = jax.tree.map(lambda a: lax.all_gather(a, axis), part)

    def take(source):
        return jax.tree.map(lambda a: lax.dynamic_index_in_dim(a, source, 0, False), gathered)

    return lax.fori_loop(
        1, lax.axis_size(axis), lambda source, state: combine(state, take(source)), take(0)
    )


def root_mean_rows(value_matrix, gain):
    mean_sq = jnp.mean(value_matrix * value_matrix, axis=-1, keepdims=True)
    return value_matrix * lax.rsqrt(mean_sq + EPS) * gain


def allowed_mask(query_count, key_start, key_count, tile_counts, tile_mask):
    tiles = tile_counts.shape[0]
    blocks = tile_mask.shape[0]
    key_pos = key_start + jnp.arange(key_count, dtype=jnp.int32)
    key_tile = key_pos // TILE_LEN
    tile_match = key_tile[:, None] == jnp.arange(tiles, dtype=jnp.int32)[None, :]
    count_here = jnp.sum(jnp.where(tile_match, tile_counts[None, :], 0), axis=1)
    slot_ok = key_pos % TILE_LEN < count_here
    query_pos = jnp.arange(query_count, dtype=jnp.int32)
    block_match = (
        query_pos[:, None] // TEXT_BLOCK == jnp.arange(blocks, dtype=jnp.int32)[None, :]
    ).astype(jnp.float32)
    row_tiles = jnp.dot(block_match, tile_mask.astype(jnp.float32), precision=lax.Precision.HIGHEST)
    seen = jnp.dot(row_tiles, tile_match.astype(jnp.float32).T, precision=lax.Precision.HIGHEST)
    return (seen > 0.5) & slot_ok[None, :]


def partial_attend(query_matrix, key_matrix, value_matrix, allowed):
    scale = query_matrix.shape[-1] ** (-0.5)
    scores = (
        jnp.einsum("ihgd,khd->ihgk", query_matrix, key_matrix, preferred_element_type=jnp.float32)
        * scale
    )
    mask = allowed[:, None, None, :]
    masked = jnp.where(mask, scores, NEG)
    top = jnp.max(masked, axis=-1)
    weights = jnp.where(mask, jnp.exp(masked - top[..., None]), 0.0)
    total = jnp.sum(weights, axis=-1)
    summed = jnp.einsum("ihgk,khd->ihgd", weights, value_matrix, precision=lax.Precision.HIGHEST)
    return (top, total, summed)


def join_parts(first, second):
    top = jnp.maximum(first[0], second[0])
    scale_first = jnp.exp(first[0] - top)
    scale_second = jnp.exp(second[0] - top)
    total = first[1] * scale_first + second[1] * scale_second
    summed = first[2] * scale_first[..., None] + second[2] * scale_second[..., None]
    return (top, total, summed)


def plain_local(
    text_states,
    vision_states,
    norm_gain,
    query_weight,
    key_value_weight,
    out_weight,
    query_gain,
    key_norm_gain,
    attn_gate,
    tile_counts,
    tile_mask,
):
    seq_count = lax.axis_size("seq")
    seq_index = lax.axis_index("seq")
    tensor_count = lax.axis_size("tensor")
    tensor_index = lax.axis_index("tensor")
    text_dev = text_states.shape[0]
    text_all = text_dev * seq_count
    vis_dev = vision_states.shape[0]
    head_size = query_gain.shape[0]
    query_local = query_weight.shape[1] // head_size
    normed = root_mean_rows(text_states.astype(jnp.float32), norm_gain.astype(jnp.float32)).astype(
        jnp.bfloat16
    )
    raw_cols, normed_cols = (
        lax.all_to_all(text_states, "seq", split_axis=1, concat_axis=0, tiled=True),
        lax.all_to_all(normed, "seq", split_axis=1, concat_axis=0, tiled=True),
    )
    rows = normed_cols
    query_raw = lax.psum_scatter(
        jnp.dot(rows, query_weight, preferred_element_type=jnp.float32),
        "seq",
        scatter_dimension=0,
        tiled=True,
    )
    query_matrix = root_mean_rows(
        query_raw.reshape(text_dev, query_local, head_size), query_gain
    ).astype(jnp.bfloat16)
    kv_full = jnp.einsum(
        "vd,jdc->jvc",
        vision_states,
        lax.all_gather(key_value_weight, "seq", axis=2, tiled=True),
        preferred_element_type=jnp.float32,
    )
    kv_local = lax.psum_scatter(kv_full, "tensor", scatter_dimension=2, tiled=True)
    kv_heads = kv_local.shape[2] // head_size
    group_size = query_local // kv_heads
    key_matrix = root_mean_rows(
        kv_local[0].reshape(vis_dev, kv_heads, head_size), key_norm_gain
    ).astype(jnp.bfloat16)
    value_matrix = kv_local[1].astype(jnp.bfloat16).reshape(vis_dev, kv_heads, head_size)
    queries_grouped = query_matrix.reshape(text_dev, kv_heads, group_size, head_size)
    query_all = lax.all_gather(queries_grouped, "seq", axis=0, tiled=True)
    allowed = allowed_mask(text_all, seq_index * vis_dev, vis_dev, tile_counts, tile_mask)
    local_parts = partial_attend(query_all, key_matrix, value_matrix.astype(jnp.float32), allowed)
    top, total, summed = combined_all(local_parts, "seq", join_parts)
    attention_all = (
        (summed / total[..., None]).reshape(text_all, query_local * head_size).astype(jnp.bfloat16)
    )
    rows_out = text_all // tensor_count
    rows = attention_all
    branch = lax.psum_scatter(
        jnp.dot(rows, out_weight, preferred_element_type=jnp.float32),
        "tensor",
        scatter_dimension=0,
        tiled=True,
    )
    residual = lax.dynamic_slice_in_dim(raw_cols, tensor_index * rows_out, rows_out, 0)
    return (residual.astype(jnp.float32) + jnp.tanh(attn_gate[0]) * branch).astype(jnp.bfloat16)


MESH = pl.DeviceIdType.MESH
RANKS = 4
CHUNKS = 4
HEAD = 128
F32, BF16 = jnp.float32, jnp.bfloat16


def landed(ref, sem):
    pltpu.make_async_copy(ref, ref, sem).wait()


def fused_kernel(
    text_ref,
    vision_ref,
    gain_ref,
    qw_hbm,
    kvw_hbm,
    ow_hbm,
    qgain_ref,
    kgain_ref,
    gate_ref,
    counts_ref,
    mask_ref,
    out_ref,
    qw,
    kvw,
    ow,
    near,
    far,
    outer_in,
    active,
    text_out,
    text_in,
    scale_out,
    scale_in,
    query_part,
    query_in,
    query_out,
    query_all,
    kv_part,
    kv_in,
    kv_done,
    att_out,
    att_in,
    rows,
    total,
    branch_out,
    branch_in,
    w_sem,
    own_send,
    outer_recv,
    near_recv,
    far_recv,
    cross_send,
    away_send,
    text_send,
    text_recv,
    scale_send,
    scale_recv,
    qp_send,
    qp_recv,
    qa_send,
    qa_recv,
    kv_send,
    kv_recv,
    done_send,
    done_recv,
    att_send,
    att_recv,
    br_send,
    br_recv,
):
    z = lax.axis_index("seq")
    t = lax.axis_index("tensor")
    core = lax.rem(t, 2)
    inner = (z == 1) | (z == 2)
    away = jnp.where(z < 2, 0, 3)
    toward = jnp.where(z < 2, 1, 2)
    across = 3 - z
    row_chunk = vision_ref.shape[0] // CHUNKS
    width = kvw.shape[2]

    def remote(src, dst, send, recv, to_z, to_t):
        return pltpu.make_async_remote_copy(
            src_ref=src,
            dst_ref=dst,
            send_sem=send,
            recv_sem=recv,
            device_id={"seq": to_z, "tensor": to_t},
            device_id_type=MESH,
        )

    loads = [
        pltpu.make_async_copy(src, dst, w_sem.at[i])
        for i, (src, dst) in enumerate(((qw_hbm, qw), (kvw_hbm, kvw), (ow_hbm, ow)))
    ]
    for load in loads:
        load.start()

    barrier = pltpu.get_barrier_semaphore()
    for d in range(1, RANKS * RANKS):
        other = lax.rem(z * RANKS + t + d, RANKS * RANKS)
        pl.semaphore_signal(
            barrier,
            inc=1,
            device_id={"seq": other // RANKS, "tensor": lax.rem(other, RANKS)},
            device_id_type=MESH,
        )

    text = text_ref[...].astype(F32)
    mean_sq = jnp.mean(text * text, axis=-1, keepdims=True)
    scale_out[...] = jnp.broadcast_to(lax.rsqrt(mean_sq + EPS), scale_out.shape)
    part = text.shape[1] // RANKS
    half = part // 2
    for b in range(RANKS):
        text_out[b] = jnp.concatenate(
            [text[:, b * part : b * part + half], text[:, b * part + half : (b + 1) * part]], axis=0
        ).astype(BF16)
    text_in[z] = text_out[z]
    scale_in[z] = scale_out[...]

    pl.semaphore_wait(barrier, RANKS * RANKS - 1)

    def text_copies(d):
        to = lax.rem(z + d, RANKS)
        return (
            remote(scale_out, scale_in.at[z], scale_send.at[d], scale_recv.at[z], to, t),
            remote(text_out.at[to], text_in.at[z], text_send.at[d], text_recv.at[z], to, t),
        )

    for d in range(1, RANKS):
        for copy in text_copies(d):
            copy.start()

    def chunk(ref, c):
        return ref.at[pl.ds(pl.multiple_of(c * row_chunk, row_chunk), row_chunk)]

    def own_outer(c):
        return remote(chunk(vision_ref, c), outer_in.at[c], own_send.at[c], outer_recv.at[c], toward, t)

    def own_inner(c):
        return remote(chunk(vision_ref, c), near.at[c], own_send.at[c], near_recv.at[c], across, t)

    def cross(c):
        return remote(outer_in.at[c], far.at[c], cross_send.at[c], far_recv.at[c], across, t)

    def away_near(c):
        return remote(active.at[c], near.at[c], away_send.at[c], near_recv.at[c], away, t)

    def away_far(c):
        return remote(far.at[c], far.at[c], away_send.at[CHUNKS + c], far_recv.at[c], away, t)

    @pl.when(inner)
    def _():
        for c in range(CHUNKS):
            own_inner(c).start()

    @pl.when(~inner)
    def _():
        for c in range(CHUNKS):
            own_outer(c).start()

    left = mask_ref[0, 0] == 1
    mine = left == (z < 2)

    for d in range(1, RANKS):
        source = lax.rem(z + d, RANKS)
        landed(scale_in.at[source], scale_recv.at[source])
        landed(text_in.at[source], text_recv.at[source])
    gain = gain_ref[...]
    pieces = []
    for b in range(RANKS):
        raw = text_in[b].astype(F32)
        raw = jnp.concatenate([raw[:8], raw[8:]], axis=1)
        pieces.append(raw * scale_in[b][:, :1] * gain)
    rows[...] = jnp.concatenate(pieces, axis=0).astype(BF16)
    loads[0].wait()
    tile = 512

    @pl.loop(0, part // tile)
    def _(n):
        cols = pl.ds(pl.multiple_of(n * tile, tile), tile)
        got = jnp.dot(rows[...], qw[:, cols], preferred_element_type=F32)
        for b in range(RANKS):
            query_part[b, :, cols] = got[8 * b : 8 * b + 8]

    def query_copy(d):
        to = lax.rem(z + d, RANKS)
        return remote(query_part.at[to], query_in.at[z], qp_send.at[d], qp_recv.at[z], to, t)

    for d in range(1, RANKS):
        query_copy(d).start()
    loads[1].wait()

    def kv_copy(i, d):
        to = lax.rem(t + d, RANKS)
        return remote(kv_part.at[i, to], kv_in.at[i, t], kv_send.at[i, d], kv_recv.at[i, t], z, to)

    def done_copy(i):
        slot = 2 * i + core
        return remote(
            kv_done.at[slot], kv_done.at[slot], done_send.at[i], done_recv.at[i], z, t + 1 - 2 * core
        )

    def finish(i):
        for d in range(1, RANKS):
            source = lax.rem(t + d, RANKS)
            landed(kv_in.at[i, source], kv_recv.at[i, source])
        got = (kv_in[i, 0] + kv_in[i, 1]) + (kv_in[i, 2] + kv_in[i, 3])
        key = root_mean_rows(got[:, :HEAD], kgain_ref[...])
        kv_done[2 * i + core] = jnp.concatenate([key, got[:, HEAD:]], axis=1).astype(BF16)
        done_copy(i).start()

    def multiply(i):
        chunk_rows = active[i]
        key = jnp.dot(chunk_rows, kvw[0], preferred_element_type=F32)
        value = jnp.dot(chunk_rows, kvw[1], preferred_element_type=F32)
        half_rows = row_chunk // 2
        for to in range(RANKS):
            r, h = (to % 2) * half_rows, (to // 2) * HEAD
            kv_part[i, to] = jnp.concatenate(
                [key[r : r + half_rows, h : h + HEAD], value[r : r + half_rows, h : h + HEAD]], axis=1
            )
        kv_in[i, t] = kv_part[i, t]
        for d in range(1, RANKS):
            kv_copy(i, d).start()

    @pl.loop(0, CHUNKS)
    def _(c):
        landed(near.at[c], near_recv.at[c])
        here = pl.ds(pl.multiple_of(c * row_chunk, row_chunk), row_chunk)

        @pl.when(inner)
        def _():
            active[c] = jnp.where(mine, vision_ref[here, :], near[c])
            away_near(c).start()
            landed(outer_in.at[c], outer_recv.at[c])
            cross(c).start()

        @pl.when(~inner)
        def _():
            active[c] = near[c]

        multiply(c)

        @pl.when(c > 0)
        def _():
            finish(c - 1)

    for d in range(1, RANKS):
        source = lax.rem(z + d, RANKS)
        landed(query_in.at[source], qp_recv.at[source])
    query_in[z] = query_part[z]
    query = (query_in[0] + query_in[1]) + (query_in[2] + query_in[3])
    heads = part // HEAD
    for side in range(2):
        query_out[side] = jnp.concatenate(
            [
                root_mean_rows(query[:, h * HEAD : (h + 1) * HEAD], qgain_ref[...])
                for h in range(side * heads // 2, (side + 1) * heads // 2)
            ],
            axis=0,
        ).astype(BF16)

    def query_send(side):
        to_t = 2 * side + z // 2
        stays = (t == z) & (t == to_t)
        k = lax.rem(z, 2)
        away_copy = remote(
            query_out.at[side], query_all.at[k], qa_send.at[side], qa_recv.at[k], t, to_t
        )
        here_copy = pltpu.make_async_copy(query_out.at[side], query_all.at[k], qa_recv.at[k])
        return stays, away_copy, here_copy

    def start_either(stays, away_copy, here_copy):
        @pl.when(stays)
        def _():
            here_copy.start()

        @pl.when(~stays)
        def _():
            away_copy.start()

    for side in range(2):
        start_either(*query_send(side))

    @pl.loop(CHUNKS, 2 * CHUNKS)
    def _(i):
        c = i - CHUNKS
        landed(far.at[c], far_recv.at[c])
        here = pl.ds(pl.multiple_of(c * row_chunk, row_chunk), row_chunk)

        @pl.when(inner)
        def _():
            away_far(c).start()
            active[i] = jnp.where(mine, outer_in[c], far[c])

        @pl.when(~inner)
        def _():
            active[i] = jnp.where(mine, vision_ref[here, :], far[c])

        multiply(i)
        finish(i - 1)

    finish(2 * CHUNKS - 1)
    for k in range(2):
        landed(query_all.at[k], qa_recv.at[k])
    for i in range(2 * CHUNKS):
        slot = 2 * i + 1 - core
        landed(kv_done.at[slot], done_recv.at[i])
    slots = 2 * vision_ref.shape[0]
    both = kv_done[...].reshape(slots, 2 * HEAD)
    queries = query_all[...].reshape(2 * query_all.shape[1], HEAD)
    scores = lax.dot_general(
        queries, both[:, :HEAD], (((1,), (1,)), ((), ())), preferred_element_type=F32
    ) * (HEAD**-0.5)
    place = lax.broadcasted_iota(jnp.int32, scores.shape, 1)
    swapped = jnp.where(place < slots // 2, place + slots // 2, place - slots // 2)
    place = jnp.where(left, swapped, place)
    valid = place < jnp.where(left, counts_ref[0], counts_ref[1])
    scores = jnp.where(valid, scores, NEG)
    top = jnp.max(scores, axis=-1, keepdims=True)
    weights = jnp.where(valid, jnp.exp(scores - top), 0.0)
    norm = jnp.sum(weights, axis=-1, keepdims=True)
    high = weights.astype(BF16)
    low = (weights - high.astype(F32)).astype(BF16)
    value = both[:, HEAD:]
    summed = jnp.dot(high, value, preferred_element_type=F32) + jnp.dot(
        low, value, preferred_element_type=F32
    )
    att_out[...] = (summed / norm).astype(BF16)

    def att_copy(d):
        to_z = lax.rem(z + d, RANKS)
        stays = (to_z == z) & (t == z)
        return (
            stays,
            remote(att_out, att_in.at[t], att_send.at[d], att_recv.at[t], to_z, z),
            pltpu.make_async_copy(att_out, att_in.at[t], att_recv.at[t]),
        )

    for d in (2, 1, 3):
        stays, away_copy, here_copy = att_copy(d)
        away_copy.start()
    start_either(*att_copy(0))
    loads[2].wait()
    for source in range(RANKS):
        landed(att_in.at[source], att_recv.at[source])
    arrived = [att_in[source].astype(F32) for source in range(RANKS)]
    group = 8
    for side in range(2):
        for j in range(group):
            column = (side * group + j) * HEAD
            rows[:, column : column + HEAD] = jnp.concatenate(
                [
                    arrived[2 * side + b // 2][(b % 2) * 64 + j * 8 : (b % 2) * 64 + j * 8 + 8]
                    for b in range(RANKS)
                ],
                axis=0,
            ).astype(BF16)

    def branch_copy(n, d):
        to = lax.rem(t + d, RANKS)
        return remote(
            branch_out.at[n, to], branch_in.at[n, t], br_send.at[n, d], br_recv.at[n, t], z, to
        )

    for n in range(2):
        parts = []
        for s in range(2):
            start = s * half + n * tile
            got = jnp.dot(rows[...], ow[:, start : start + tile], preferred_element_type=F32)
            total[:, start : start + tile] = got
            parts.append(got)
        for to in range(RANKS):
            branch_out[n, to] = jnp.concatenate(
                [got[8 * to : 8 * to + 8] for got in parts], axis=0
            ).astype(BF16)
        for d in (2, 1, 3):
            branch_copy(n, d).start()

    gate = jnp.tanh(jnp.full((8, tile), gate_ref[0], F32))
    residual = text_in[t].astype(F32)
    own_rows = pl.ds(pl.multiple_of(8 * t, 8), 8)
    for n in range(2):
        for d in range(1, RANKS):
            source = lax.rem(t + d, RANKS)
            landed(branch_in.at[n, source], br_recv.at[n, source])
        others = []
        for d in range(1, RANKS):
            others.append(branch_in[n, lax.rem(t + d, RANKS)].astype(F32))
        other = (others[0] + others[1]) + others[2]
        for s in range(2):
            start = s * half + n * tile
            branch = total[own_rows, start : start + tile] + other[8 * s : 8 * s + 8]
            base = residual[8 * s : 8 * s + 8, n * tile : (n + 1) * tile]
            out_ref[:, start : start + tile] = (base + gate * branch).astype(BF16)

    for d in range(1, RANKS):
        for copy in text_copies(d):
            copy.wait_send()
        query_copy(d).wait_send()
        att_copy(d)[1].wait_send()
        for n in range(2):
            branch_copy(n, d).wait_send()
    stays, away_copy, here_copy = att_copy(0)

    @pl.when(~stays)
    def _():
        away_copy.wait_send()

    for side in range(2):
        q_stays, q_away, q_here = query_send(side)

        @pl.when(~q_stays)
        def _():
            q_away.wait_send()

    @pl.loop(0, CHUNKS)
    def _(c):
        own_inner(c).wait_send()

        @pl.when(inner)
        def _():
            cross(c).wait_send()
            away_near(c).wait_send()
            away_far(c).wait_send()

    @pl.loop(0, 2 * CHUNKS)
    def _(i):
        for d in range(1, RANKS):
            kv_copy(i, d).wait_send()
        done_copy(i).wait_send()


def fused_fits(text_states, vision_states, query_weight, key_value_weight, out_weight, query_gain, tile_counts, tile_mask):
    return (
        lax.axis_size("seq") == RANKS
        and lax.axis_size("tensor") == RANKS
        and tile_mask.shape == (1, 2)
        and tile_counts.shape == (2,)
        and text_states.shape == (8, 8192)
        and vision_states.shape == (256, 2048)
        and query_weight.shape == (2048, 2048)
        and out_weight.shape == (2048, 2048)
        and key_value_weight.shape == (2, 2048, 256)
        and query_gain.shape == (HEAD,)
    )


def fused_local(
    text_states,
    vision_states,
    norm_gain,
    query_weight,
    key_value_weight,
    out_weight,
    query_gain,
    key_norm_gain,
    attn_gate,
    tile_counts,
    tile_mask,
):
    part = query_weight.shape[0]
    tokens, slots = text_states.shape[0], vision_states.shape[0]
    chunk = slots // CHUNKS
    z = lax.axis_index("seq")
    gain = lax.dynamic_slice_in_dim(norm_gain, z * part, part).astype(F32).reshape(1, part)
    vmem = pl.BlockSpec(memory_space=pltpu.VMEM)
    smem = pl.BlockSpec(memory_space=pltpu.SMEM)
    hbm = pl.BlockSpec(memory_space=pl.ANY)
    block = pltpu.VMEM((CHUNKS, chunk, part), BF16)
    dma = pltpu.SemaphoreType.DMA
    return pl.pallas_call(
        fused_kernel,
        out_shape=jax.ShapeDtypeStruct((tokens, part), BF16),
        in_specs=[vmem, vmem, vmem, hbm, hbm, hbm, vmem, vmem, smem, smem, smem],
        out_specs=vmem,
        scratch_shapes=[
            pltpu.VMEM(query_weight.shape, BF16),
            pltpu.VMEM(key_value_weight.shape, BF16),
            pltpu.VMEM(out_weight.shape, BF16),
            block,
            block,
            block,
            pltpu.VMEM((2 * CHUNKS, chunk, part), BF16),
            pltpu.VMEM((RANKS, 16, part // 2), BF16),
            pltpu.VMEM((RANKS, 16, part // 2), BF16),
            pltpu.VMEM((8, HEAD), F32),
            pltpu.VMEM((RANKS, 8, HEAD), F32),
            pltpu.VMEM((RANKS, 8, part), F32),
            pltpu.VMEM((RANKS, 8, part), F32),
            pltpu.VMEM((2, 64, HEAD), BF16),
            pltpu.VMEM((2, 64, HEAD), BF16),
            pltpu.VMEM((2 * CHUNKS, RANKS, chunk // 2, 2 * HEAD), F32),
            pltpu.VMEM((2 * CHUNKS, RANKS, chunk // 2, 2 * HEAD), F32),
            pltpu.VMEM((4 * CHUNKS, chunk // 2, 2 * HEAD), BF16),
            pltpu.VMEM((128, HEAD), BF16),
            pltpu.VMEM((RANKS, 128, HEAD), BF16),
            pltpu.VMEM((32, part), BF16),
            pltpu.VMEM((32, part), F32),
            pltpu.VMEM((2, RANKS, 16, 512), BF16),
            pltpu.VMEM((2, RANKS, 16, 512), BF16),
            dma((3,)),
            dma((CHUNKS,)),
            dma((CHUNKS,)),
            dma((CHUNKS,)),
            dma((CHUNKS,)),
            dma((CHUNKS,)),
            dma((2 * CHUNKS,)),
            dma((RANKS,)),
            dma((RANKS,)),
            dma((RANKS,)),
            dma((RANKS,)),
            dma((RANKS,)),
            dma((RANKS,)),
            dma((2,)),
            dma((2,)),
            dma((2 * CHUNKS, RANKS)),
            dma((2 * CHUNKS, RANKS)),
            dma((2 * CHUNKS,)),
            dma((2 * CHUNKS,)),
            dma((RANKS,)),
            dma((RANKS,)),
            dma((2, RANKS)),
            dma((2, RANKS)),
        ],
        compiler_params=pltpu.CompilerParams(
            collective_id=0, has_side_effects=True, vmem_limit_bytes=56 * 1024 * 1024
        ),
    )(
        text_states,
        vision_states,
        gain,
        query_weight,
        key_value_weight,
        out_weight,
        query_gain.reshape(1, HEAD),
        key_norm_gain.reshape(1, HEAD),
        attn_gate,
        tile_counts,
        tile_mask,
    )


def local(*args):
    text, vision, _, query_weight, kv_weight, out_weight, query_gain, _, _, counts, mask = args
    if fused_fits(text, vision, query_weight, kv_weight, out_weight, query_gain, counts, mask):
        return fused_local(*args)
    return plain_local(*args)


def solution(mesh):
    return jax.shard_map(
        local,
        mesh=mesh,
        in_specs=(
            P(("groups", "seq"), None),
            P(("groups", "seq"), "tensor"),
            P(),
            P("seq", "tensor"),
            P(None, "tensor", "seq"),
            P("tensor", "seq"),
            P(),
            P(),
            P(),
            P("groups"),
            P("groups", None),
        ),
        out_specs=P(("groups", "tensor"), "seq"),
        check_vma=False,
    )
```

```python
import jax
import jax.numpy as jnp
from jax import lax
from jax.experimental import pallas as pl
from jax.experimental.pallas import tpu as pltpu
from jax.sharding import PartitionSpec as P

TILE_LEN = 512
TEXT_BLOCK = 32


EPS = 1e-05
NEG = -1e30


def combined_all(part, axis, combine):
    gathered = jax.tree.map(lambda a: lax.all_gather(a, axis), part)

    def take(source):
        return jax.tree.map(lambda a: lax.dynamic_index_in_dim(a, source, 0, False), gathered)

    return lax.fori_loop(
        1, lax.axis_size(axis), lambda source, state: combine(state, take(source)), take(0)
    )


def root_mean_rows(value_matrix, gain):
    mean_sq = jnp.mean(value_matrix * value_matrix, axis=-1, keepdims=True)
    return value_matrix * lax.rsqrt(mean_sq + EPS) * gain


def allowed_mask(query_count, key_start, key_count, tile_counts, tile_mask):
    tiles = tile_counts.shape[0]
    blocks = tile_mask.shape[0]
    key_pos = key_start + jnp.arange(key_count, dtype=jnp.int32)
    key_tile = key_pos // TILE_LEN
    tile_match = key_tile[:, None] == jnp.arange(tiles, dtype=jnp.int32)[None, :]
    count_here = jnp.sum(jnp.where(tile_match, tile_counts[None, :], 0), axis=1)
    slot_ok = key_pos % TILE_LEN < count_here
    query_pos = jnp.arange(query_count, dtype=jnp.int32)
    block_match = (
        query_pos[:, None] // TEXT_BLOCK == jnp.arange(blocks, dtype=jnp.int32)[None, :]
    ).astype(jnp.float32)
    row_tiles = jnp.dot(block_match, tile_mask.astype(jnp.float32), precision=lax.Precision.HIGHEST)
    seen = jnp.dot(row_tiles, tile_match.astype(jnp.float32).T, precision=lax.Precision.HIGHEST)
    return (seen > 0.5) & slot_ok[None, :]


def partial_attend(query_matrix, key_matrix, value_matrix, allowed):
    scale = query_matrix.shape[-1] ** (-0.5)
    scores = (
        jnp.einsum("ihgd,khd->ihgk", query_matrix, key_matrix, preferred_element_type=jnp.float32)
        * scale
    )
    mask = allowed[:, None, None, :]
    masked = jnp.where(mask, scores, NEG)
    top = jnp.max(masked, axis=-1)
    weights = jnp.where(mask, jnp.exp(masked - top[..., None]), 0.0)
    total = jnp.sum(weights, axis=-1)
    summed = jnp.einsum("ihgk,khd->ihgd", weights, value_matrix, precision=lax.Precision.HIGHEST)
    return (top, total, summed)


def join_parts(first, second):
    top = jnp.maximum(first[0], second[0])
    scale_first = jnp.exp(first[0] - top)
    scale_second = jnp.exp(second[0] - top)
    total = first[1] * scale_first + second[1] * scale_second
    summed = first[2] * scale_first[..., None] + second[2] * scale_second[..., None]
    return (top, total, summed)


def plain_local(
    text_states,
    vision_states,
    norm_gain,
    query_weight,
    key_value_weight,
    out_weight,
    query_gain,
    key_norm_gain,
    attn_gate,
    tile_counts,
    tile_mask,
):
    seq_count = lax.axis_size("seq")
    seq_index = lax.axis_index("seq")
    tensor_count = lax.axis_size("tensor")
    tensor_index = lax.axis_index("tensor")
    text_dev = text_states.shape[0]
    text_all = text_dev * seq_count
    vis_dev = vision_states.shape[0]
    head_size = query_gain.shape[0]
    query_local = query_weight.shape[1] // head_size
    normed = root_mean_rows(text_states.astype(jnp.float32), norm_gain.astype(jnp.float32)).astype(
        jnp.bfloat16
    )
    raw_cols, normed_cols = (
        lax.all_to_all(text_states, "seq", split_axis=1, concat_axis=0, tiled=True),
        lax.all_to_all(normed, "seq", split_axis=1, concat_axis=0, tiled=True),
    )
    rows = normed_cols
    query_raw = lax.psum_scatter(
        jnp.dot(rows, query_weight, preferred_element_type=jnp.float32),
        "seq",
        scatter_dimension=0,
        tiled=True,
    )
    query_matrix = root_mean_rows(
        query_raw.reshape(text_dev, query_local, head_size), query_gain
    ).astype(jnp.bfloat16)
    kv_full = jnp.einsum(
        "vd,jdc->jvc",
        vision_states,
        lax.all_gather(key_value_weight, "seq", axis=2, tiled=True),
        preferred_element_type=jnp.float32,
    )
    kv_local = lax.psum_scatter(kv_full, "tensor", scatter_dimension=2, tiled=True)
    kv_heads = kv_local.shape[2] // head_size
    group_size = query_local // kv_heads
    key_matrix = root_mean_rows(
        kv_local[0].reshape(vis_dev, kv_heads, head_size), key_norm_gain
    ).astype(jnp.bfloat16)
    value_matrix = kv_local[1].astype(jnp.bfloat16).reshape(vis_dev, kv_heads, head_size)
    queries_grouped = query_matrix.reshape(text_dev, kv_heads, group_size, head_size)
    query_all = lax.all_gather(queries_grouped, "seq", axis=0, tiled=True)
    allowed = allowed_mask(text_all, seq_index * vis_dev, vis_dev, tile_counts, tile_mask)
    local_parts = partial_attend(query_all, key_matrix, value_matrix.astype(jnp.float32), allowed)
    top, total, summed = combined_all(local_parts, "seq", join_parts)
    attention_all = (
        (summed / total[..., None]).reshape(text_all, query_local * head_size).astype(jnp.bfloat16)
    )
    rows_out = text_all // tensor_count
    rows = attention_all
    branch = lax.psum_scatter(
        jnp.dot(rows, out_weight, preferred_element_type=jnp.float32),
        "tensor",
        scatter_dimension=0,
        tiled=True,
    )
    residual = lax.dynamic_slice_in_dim(raw_cols, tensor_index * rows_out, rows_out, 0)
    return (residual.astype(jnp.float32) + jnp.tanh(attn_gate[0]) * branch).astype(jnp.bfloat16)


MESH = pl.DeviceIdType.MESH
RANKS = 4
CHUNKS = 4
SUBS = 2
SENDS = CHUNKS * SUBS
AHEAD = 3
HEAD = 128
F32, BF16 = jnp.float32, jnp.bfloat16


def landed(ref, sem):
    pltpu.make_async_copy(ref, ref, sem).wait()


def fused_kernel(
    text_ref,
    vision_ref,
    gain_ref,
    qw_hbm,
    kvw_hbm,
    ow_hbm,
    qgain_ref,
    kgain_ref,
    gate_ref,
    counts_ref,
    mask_ref,
    out_ref,
    qw,
    kvw,
    ow,
    near,
    far,
    outer_in,
    active,
    text_out,
    text_in,
    scale_out,
    scale_in,
    query_part,
    query_in,
    mid_out,
    mid_in,
    last_out,
    last_in,
    query_out,
    query_all,
    kv_part,
    kv_in,
    kv_done,
    att_out,
    att_in,
    rows,
    total,
    branch_out,
    branch_in,
    w_sem,
    own_send,
    outer_recv,
    near_recv,
    far_recv,
    cross_send,
    away_send,
    text_send,
    text_recv,
    scale_send,
    scale_recv,
    qp_send,
    qp_recv,
    mid_sem,
    last_sem,
    qa_send,
    qa_recv,
    kv_send,
    kv_recv,
    done_send,
    done_recv,
    att_send,
    att_recv,
    br_send,
    br_recv,
):
    z = lax.axis_index("seq")
    t = lax.axis_index("tensor")
    core = lax.rem(t, 2)
    inner = (z == 1) | (z == 2)
    away = jnp.where(z < 2, 0, 3)
    toward = jnp.where(z < 2, 1, 2)
    across = 3 - z
    row_chunk = vision_ref.shape[0] // CHUNKS
    sub_rows = row_chunk // SUBS

    def remote(src, dst, send, recv, to_z, to_t):
        return pltpu.make_async_remote_copy(
            src_ref=src,
            dst_ref=dst,
            send_sem=send,
            recv_sem=recv,
            device_id={"seq": to_z, "tensor": to_t},
            device_id_type=MESH,
        )

    loads = [
        pltpu.make_async_copy(src, dst, w_sem.at[i])
        for i, (src, dst) in enumerate(((qw_hbm, qw), (kvw_hbm, kvw), (ow_hbm, ow)))
    ]
    for load in loads:
        load.start()

    barrier = pltpu.get_barrier_semaphore()
    for d in range(1, RANKS * RANKS):
        other = lax.rem(z * RANKS + t + d, RANKS * RANKS)
        pl.semaphore_signal(
            barrier,
            inc=1,
            device_id={"seq": other // RANKS, "tensor": lax.rem(other, RANKS)},
            device_id_type=MESH,
        )

    text = text_ref[...].astype(F32)
    mean_sq = jnp.mean(text * text, axis=-1, keepdims=True)
    scale_out[...] = jnp.broadcast_to(lax.rsqrt(mean_sq + EPS), scale_out.shape)
    part = text.shape[1] // RANKS
    half = part // 2
    for b in range(RANKS):
        text_out[b] = jnp.concatenate(
            [text[:, b * part : b * part + half], text[:, b * part + half : (b + 1) * part]], axis=0
        ).astype(BF16)
    text_in[z] = text_out[z]
    scale_in[z] = scale_out[...]

    pl.semaphore_wait(barrier, RANKS * RANKS - 1)

    def text_copies(d):
        to = lax.rem(z + d, RANKS)
        return (
            remote(scale_out, scale_in.at[z], scale_send.at[d], scale_recv.at[z], to, t),
            remote(text_out.at[to], text_in.at[z], text_send.at[d], text_recv.at[z], to, t),
        )

    for d in range(1, RANKS):
        for copy in text_copies(d):
            copy.start()

    def rows_of(u):
        return pl.ds(pl.multiple_of(u * sub_rows, sub_rows), sub_rows)

    def sub(ref, u):
        return ref.at[rows_of(u)]

    def own_outer(u):
        return remote(
            sub(vision_ref, u), sub(outer_in, u), own_send.at[u], outer_recv.at[u], toward, t
        )

    def own_inner(u):
        return remote(sub(vision_ref, u), sub(near, u), own_send.at[u], near_recv.at[u], across, t)

    def cross(u):
        return remote(sub(outer_in, u), sub(far, u), cross_send.at[u], far_recv.at[u], across, t)

    def away_near(u):
        return remote(sub(active, u), sub(near, u), away_send.at[u], near_recv.at[u], away, t)

    def away_far(u):
        return remote(sub(far, u), sub(far, u), away_send.at[SENDS + u], far_recv.at[u], away, t)

    def send_across(m):
        @pl.when(m < SENDS)
        def _():
            own_inner(m).start()

        @pl.when((m >= SENDS) & (m < 2 * SENDS))
        def _():
            u = m - SENDS
            landed(sub(outer_in, u), outer_recv.at[u])
            cross(u).start()

    @pl.when(inner)
    def _():
        for u in range(AHEAD):
            own_inner(u).start()

    @pl.when(~inner)
    def _():
        for u in range(SENDS):
            own_outer(u).start()

    left = mask_ref[0, 0] == 1
    mine = left == (z < 2)

    tile = 512

    def take_text():
        for d in range(1, RANKS):
            source = lax.rem(z + d, RANKS)
            landed(scale_in.at[source], scale_recv.at[source])
            landed(text_in.at[source], text_recv.at[source])
        gain = gain_ref[pl.ds(pl.multiple_of(z * part, part), part)].astype(F32).reshape(1, part)
        pieces = []
        for b in range(RANKS):
            raw = text_in[b].astype(F32)
            raw = jnp.concatenate([raw[:8], raw[8:]], axis=1)
            pieces.append(raw * scale_in[b][:, :1] * gain)
        rows[...] = jnp.concatenate(pieces, axis=0).astype(BF16)
        loads[0].wait()

    def query_tile(n):
        cols = slice(n * tile, (n + 1) * tile)
        got = jnp.dot(rows[...], qw[:, cols], preferred_element_type=F32)
        for b in range(RANKS):
            query_part[b, :, cols] = got[8 * b : 8 * b + 8]

    outer_blocks = (toward, 3 - toward, 3 - z)

    def query_inward(n):
        b = outer_blocks[n]
        return remote(query_part.at[b], query_in.at[b], qp_send.at[n], qp_recv.at[b], toward, t)

    def query_across():
        return remote(mid_out, mid_in, mid_sem.at[0], mid_sem.at[1], across, t)

    def query_outward():
        return remote(last_out, last_in, last_sem.at[0], last_sem.at[1], away, t)

    loads[1].wait()

    def kv_copy(i, d):
        to = lax.rem(t + d, RANKS)
        return remote(kv_part.at[i, to], kv_in.at[i, t], kv_send.at[i, d], kv_recv.at[i, t], z, to)

    def done_copy(i):
        slot = 2 * i + core
        return remote(
            kv_done.at[slot], kv_done.at[slot], done_send.at[i], done_recv.at[i], z, t + 1 - 2 * core
        )

    def finish(i):
        for d in range(1, RANKS):
            source = lax.rem(t + d, RANKS)
            landed(kv_in.at[i, source], kv_recv.at[i, source])
        got = (kv_in[i, 0] + kv_in[i, 1]) + (kv_in[i, 2] + kv_in[i, 3])
        key = root_mean_rows(got[:, :HEAD], kgain_ref[...])
        kv_done[2 * i + core] = jnp.concatenate([key, got[:, HEAD:]], axis=1).astype(BF16)
        done_copy(i).start()

    def multiply(i):
        chunk_rows = active[pl.ds(pl.multiple_of(i * row_chunk, row_chunk), row_chunk), :]
        key = jnp.dot(chunk_rows, kvw[0], preferred_element_type=F32)
        value = jnp.dot(chunk_rows, kvw[1], preferred_element_type=F32)
        half_rows = row_chunk // 2
        for to in range(RANKS):
            r, h = (to % 2) * half_rows, (to // 2) * HEAD
            kv_part[i, to] = jnp.concatenate(
                [key[r : r + half_rows, h : h + HEAD], value[r : r + half_rows, h : h + HEAD]], axis=1
            )
        kv_in[i, t] = kv_part[i, t]
        for d in range(1, RANKS):
            kv_copy(i, d).start()

    @pl.loop(0, CHUNKS)
    def _(c):
        for s in range(SUBS):
            u = c * SUBS + s
            here = rows_of(u)
            landed(sub(near, u), near_recv.at[u])

            @pl.when(inner)
            def _():
                active[here, :] = jnp.where(mine, vision_ref[here, :], near[here, :])
                away_near(u).start()
                send_across(u + AHEAD)

            @pl.when(~inner)
            def _():
                active[here, :] = near[here, :]

        multiply(c)

        @pl.when(c > 0)
        def _():
            finish(c - 1)

        @pl.when(c == 1)
        def _():
            take_text()
            query_tile(0)
            query_tile(1)

        @pl.when(c == 2)
        def _():
            query_tile(2)
            query_tile(3)

            @pl.when(~inner)
            def _():
                for n in range(3):
                    query_inward(n).start()

        @pl.when((c == 3) & inner)
        def _():
            for b in (z, across, 3 - away):
                landed(query_in.at[b], qp_recv.at[b])
            for n, b in enumerate((across, 3 - away)):
                mid_out[n] = query_part[b] + query_in[b]
            query_across().start()

    heads = part // HEAD

    def take_query(query):
        for side in range(2):
            query_out[side] = jnp.concatenate(
                [
                    root_mean_rows(query[:, h * HEAD : (h + 1) * HEAD], qgain_ref[...])
                    for h in range(side * heads // 2, (side + 1) * heads // 2)
                ],
                axis=0,
            ).astype(BF16)
        for side in range(2):
            start_either(*query_send(side))

    def query_send(side):
        to_t = 2 * side + z // 2
        stays = (t == z) & (t == to_t)
        k = lax.rem(z, 2)
        away_copy = remote(
            query_out.at[side], query_all.at[k], qa_send.at[side], qa_recv.at[k], t, to_t
        )
        here_copy = pltpu.make_async_copy(query_out.at[side], query_all.at[k], qa_recv.at[k])
        return stays, away_copy, here_copy

    def start_either(stays, away_copy, here_copy):
        @pl.when(stays)
        def _():
            here_copy.start()

        @pl.when(~stays)
        def _():
            away_copy.start()

    @pl.loop(CHUNKS, 2 * CHUNKS)
    def _(i):
        for s in range(SUBS):
            u = (i - CHUNKS) * SUBS + s
            here = rows_of(u)
            to = rows_of(u + SENDS)
            landed(sub(far, u), far_recv.at[u])

            @pl.when(inner)
            def _():
                away_far(u).start()
                send_across(u + SENDS + AHEAD)
                active[to, :] = jnp.where(mine, outer_in[here, :], far[here, :])

            @pl.when(~inner)
            def _():
                active[to, :] = jnp.where(mine, vision_ref[here, :], far[here, :])

        multiply(i)
        finish(i - 1)

        @pl.when((i == CHUNKS + 1) & inner)
        def _():
            landed(mid_in, mid_sem.at[1])
            last_out[...] = query_part[away] + mid_in[1]
            query_outward().start()
            take_query((query_part[z] + query_in[z]) + mid_in[0])

        @pl.when((i == CHUNKS + 2) & ~inner)
        def _():
            landed(last_in, last_sem.at[1])
            take_query(query_part[z] + last_in[...])

    finish(2 * CHUNKS - 1)
    for k in range(2):
        landed(query_all.at[k], qa_recv.at[k])
    for i in range(2 * CHUNKS):
        slot = 2 * i + 1 - core
        landed(kv_done.at[slot], done_recv.at[i])
    slots = 2 * vision_ref.shape[0]
    both = kv_done[...].reshape(slots, 2 * HEAD)
    queries = query_all[...].reshape(2 * query_all.shape[1], HEAD)
    scores = lax.dot_general(
        queries, both[:, :HEAD], (((1,), (1,)), ((), ())), preferred_element_type=F32
    ) * (HEAD**-0.5)
    place = lax.broadcasted_iota(jnp.int32, scores.shape, 1)
    swapped = jnp.where(place < slots // 2, place + slots // 2, place - slots // 2)
    place = jnp.where(left, swapped, place)
    valid = place < jnp.where(left, counts_ref[0], counts_ref[1])
    scores = jnp.where(valid, scores, NEG)
    top = jnp.max(scores, axis=-1, keepdims=True)
    weights = jnp.where(valid, jnp.exp(scores - top), 0.0)
    norm = jnp.sum(weights, axis=-1, keepdims=True)
    high = weights.astype(BF16)
    low = (weights - high.astype(F32)).astype(BF16)
    value = both[:, HEAD:]
    summed = jnp.dot(high, value, preferred_element_type=F32) + jnp.dot(
        low, value, preferred_element_type=F32
    )
    att_out[...] = (summed / norm).astype(BF16)

    def att_copy(d):
        to_z = lax.rem(z + d, RANKS)
        stays = (to_z == z) & (t == z)
        return (
            stays,
            remote(att_out, att_in.at[t], att_send.at[d], att_recv.at[t], to_z, z),
            pltpu.make_async_copy(att_out, att_in.at[t], att_recv.at[t]),
        )

    for d in (2, 1, 3):
        stays, away_copy, here_copy = att_copy(d)
        away_copy.start()
    start_either(*att_copy(0))
    loads[2].wait()
    for source in range(RANKS):
        landed(att_in.at[source], att_recv.at[source])
    arrived = [att_in[source].astype(F32) for source in range(RANKS)]
    group = 8
    for side in range(2):
        for j in range(group):
            column = (side * group + j) * HEAD
            rows[:, column : column + HEAD] = jnp.concatenate(
                [
                    arrived[2 * side + b // 2][(b % 2) * 64 + j * 8 : (b % 2) * 64 + j * 8 + 8]
                    for b in range(RANKS)
                ],
                axis=0,
            ).astype(BF16)

    def branch_copy(n, d):
        to = lax.rem(t + d, RANKS)
        return remote(
            branch_out.at[n, to], branch_in.at[n, t], br_send.at[n, d], br_recv.at[n, t], z, to
        )

    for n in range(2):
        parts = []
        for s in range(2):
            start = s * half + n * tile
            got = jnp.dot(rows[...], ow[:, start : start + tile], preferred_element_type=F32)
            total[:, start : start + tile] = got
            parts.append(got)
        for to in range(RANKS):
            branch_out[n, to] = jnp.concatenate(
                [got[8 * to : 8 * to + 8] for got in parts], axis=0
            ).astype(BF16)
        for d in (2, 1, 3):
            branch_copy(n, d).start()

    gate = jnp.tanh(jnp.full((8, tile), gate_ref[0], F32))
    residual = text_in[t].astype(F32)
    own_rows = pl.ds(pl.multiple_of(8 * t, 8), 8)
    for n in range(2):
        for d in range(1, RANKS):
            source = lax.rem(t + d, RANKS)
            landed(branch_in.at[n, source], br_recv.at[n, source])
        others = []
        for d in range(1, RANKS):
            others.append(branch_in[n, lax.rem(t + d, RANKS)].astype(F32))
        other = (others[0] + others[1]) + others[2]
        for s in range(2):
            start = s * half + n * tile
            branch = total[own_rows, start : start + tile] + other[8 * s : 8 * s + 8]
            base = residual[8 * s : 8 * s + 8, n * tile : (n + 1) * tile]
            out_ref[:, start : start + tile] = (base + gate * branch).astype(BF16)

    for d in range(1, RANKS):
        for copy in text_copies(d):
            copy.wait_send()
        att_copy(d)[1].wait_send()
        for n in range(2):
            branch_copy(n, d).wait_send()
    stays, away_copy, here_copy = att_copy(0)

    @pl.when(~stays)
    def _():
        away_copy.wait_send()

    for side in range(2):
        q_stays, q_away, q_here = query_send(side)

        @pl.when(~q_stays)
        def _():
            q_away.wait_send()

    @pl.when(inner)
    def _():
        query_across().wait_send()
        query_outward().wait_send()

    @pl.when(~inner)
    def _():
        for n in range(3):
            query_inward(n).wait_send()

    @pl.loop(0, SENDS)
    def _(u):
        own_inner(u).wait_send()

        @pl.when(inner)
        def _():
            cross(u).wait_send()
            away_near(u).wait_send()
            away_far(u).wait_send()

    @pl.loop(0, 2 * CHUNKS)
    def _(i):
        for d in range(1, RANKS):
            kv_copy(i, d).wait_send()
        done_copy(i).wait_send()


def fused_fits(text_states, vision_states, query_weight, key_value_weight, out_weight, query_gain, tile_counts, tile_mask):
    return (
        lax.axis_size("seq") == RANKS
        and lax.axis_size("tensor") == RANKS
        and tile_mask.shape == (1, 2)
        and tile_counts.shape == (2,)
        and text_states.shape == (8, 8192)
        and vision_states.shape == (256, 2048)
        and query_weight.shape == (2048, 2048)
        and out_weight.shape == (2048, 2048)
        and key_value_weight.shape == (2, 2048, 256)
        and query_gain.shape == (HEAD,)
    )


def fused_local(
    text_states,
    vision_states,
    norm_gain,
    query_weight,
    key_value_weight,
    out_weight,
    query_gain,
    key_norm_gain,
    attn_gate,
    tile_counts,
    tile_mask,
):
    part = query_weight.shape[0]
    tokens, slots = text_states.shape[0], vision_states.shape[0]
    chunk = slots // CHUNKS
    vmem = pl.BlockSpec(memory_space=pltpu.VMEM)
    smem = pl.BlockSpec(memory_space=pltpu.SMEM)
    hbm = pl.BlockSpec(memory_space=pl.ANY)
    block = pltpu.VMEM((slots, part), BF16)
    dma = pltpu.SemaphoreType.DMA
    return pl.pallas_call(
        fused_kernel,
        out_shape=jax.ShapeDtypeStruct((tokens, part), BF16),
        in_specs=[vmem, vmem, vmem, hbm, hbm, hbm, vmem, vmem, smem, smem, smem],
        out_specs=vmem,
        scratch_shapes=[
            pltpu.VMEM(query_weight.shape, BF16),
            pltpu.VMEM(key_value_weight.shape, BF16),
            pltpu.VMEM(out_weight.shape, BF16),
            block,
            block,
            block,
            pltpu.VMEM((2 * slots, part), BF16),
            pltpu.VMEM((RANKS, 16, part // 2), BF16),
            pltpu.VMEM((RANKS, 16, part // 2), BF16),
            pltpu.VMEM((8, HEAD), F32),
            pltpu.VMEM((RANKS, 8, HEAD), F32),
            pltpu.VMEM((RANKS, 8, part), F32),
            pltpu.VMEM((RANKS, 8, part), F32),
            pltpu.VMEM((2, 8, part), F32),
            pltpu.VMEM((2, 8, part), F32),
            pltpu.VMEM((8, part), F32),
            pltpu.VMEM((8, part), F32),
            pltpu.VMEM((2, 64, HEAD), BF16),
            pltpu.VMEM((2, 64, HEAD), BF16),
            pltpu.VMEM((2 * CHUNKS, RANKS, chunk // 2, 2 * HEAD), F32),
            pltpu.VMEM((2 * CHUNKS, RANKS, chunk // 2, 2 * HEAD), F32),
            pltpu.VMEM((4 * CHUNKS, chunk // 2, 2 * HEAD), BF16),
            pltpu.VMEM((128, HEAD), BF16),
            pltpu.VMEM((RANKS, 128, HEAD), BF16),
            pltpu.VMEM((32, part), BF16),
            pltpu.VMEM((32, part), F32),
            pltpu.VMEM((2, RANKS, 16, 512), BF16),
            pltpu.VMEM((2, RANKS, 16, 512), BF16),
            dma((3,)),
            dma((SENDS,)),
            dma((SENDS,)),
            dma((SENDS,)),
            dma((SENDS,)),
            dma((SENDS,)),
            dma((2 * SENDS,)),
            dma((RANKS,)),
            dma((RANKS,)),
            dma((RANKS,)),
            dma((RANKS,)),
            dma((RANKS,)),
            dma((RANKS,)),
            dma((2,)),
            dma((2,)),
            dma((2,)),
            dma((2,)),
            dma((2 * CHUNKS, RANKS)),
            dma((2 * CHUNKS, RANKS)),
            dma((2 * CHUNKS,)),
            dma((2 * CHUNKS,)),
            dma((RANKS,)),
            dma((RANKS,)),
            dma((2, RANKS)),
            dma((2, RANKS)),
        ],
        compiler_params=pltpu.CompilerParams(
            collective_id=0, has_side_effects=True, vmem_limit_bytes=56 * 1024 * 1024
        ),
    )(
        text_states,
        vision_states,
        norm_gain,
        query_weight,
        key_value_weight,
        out_weight,
        query_gain.reshape(1, HEAD),
        key_norm_gain.reshape(1, HEAD),
        attn_gate,
        tile_counts,
        tile_mask,
    )


def local(*args):
    text, vision, _, query_weight, kv_weight, out_weight, query_gain, _, _, counts, mask = args
    if fused_fits(text, vision, query_weight, kv_weight, out_weight, query_gain, counts, mask):
        return fused_local(*args)
    return plain_local(*args)


def solution(mesh):
    return jax.shard_map(
        local,
        mesh=mesh,
        in_specs=(
            P(("groups", "seq"), None),
            P(("groups", "seq"), "tensor"),
            P(),
            P("seq", "tensor"),
            P(None, "tensor", "seq"),
            P("tensor", "seq"),
            P(),
            P(),
            P(),
            P("groups"),
            P("groups", None),
        ),
        out_specs=P(("groups", "tensor"), "seq"),
        check_vma=False,
    )
```

```python
import jax
import jax.numpy as jnp
from jax import lax
from jax.experimental import pallas as pl
from jax.experimental.pallas import tpu as pltpu
from jax.sharding import PartitionSpec as P

TILE_LEN = 512
TEXT_BLOCK = 32


EPS = 1e-05
NEG = -1e30


def combined_all(part, axis, combine):
    gathered = jax.tree.map(lambda a: lax.all_gather(a, axis), part)

    def take(source):
        return jax.tree.map(lambda a: lax.dynamic_index_in_dim(a, source, 0, False), gathered)

    return lax.fori_loop(
        1, lax.axis_size(axis), lambda source, state: combine(state, take(source)), take(0)
    )


def root_mean_rows(value_matrix, gain):
    mean_sq = jnp.mean(value_matrix * value_matrix, axis=-1, keepdims=True)
    return value_matrix * lax.rsqrt(mean_sq + EPS) * gain


def allowed_mask(query_count, key_start, key_count, tile_counts, tile_mask):
    tiles = tile_counts.shape[0]
    blocks = tile_mask.shape[0]
    key_pos = key_start + jnp.arange(key_count, dtype=jnp.int32)
    key_tile = key_pos // TILE_LEN
    tile_match = key_tile[:, None] == jnp.arange(tiles, dtype=jnp.int32)[None, :]
    count_here = jnp.sum(jnp.where(tile_match, tile_counts[None, :], 0), axis=1)
    slot_ok = key_pos % TILE_LEN < count_here
    query_pos = jnp.arange(query_count, dtype=jnp.int32)
    block_match = (
        query_pos[:, None] // TEXT_BLOCK == jnp.arange(blocks, dtype=jnp.int32)[None, :]
    ).astype(jnp.float32)
    row_tiles = jnp.dot(block_match, tile_mask.astype(jnp.float32), precision=lax.Precision.HIGHEST)
    seen = jnp.dot(row_tiles, tile_match.astype(jnp.float32).T, precision=lax.Precision.HIGHEST)
    return (seen > 0.5) & slot_ok[None, :]


def partial_attend(query_matrix, key_matrix, value_matrix, allowed):
    scale = query_matrix.shape[-1] ** (-0.5)
    scores = (
        jnp.einsum("ihgd,khd->ihgk", query_matrix, key_matrix, preferred_element_type=jnp.float32)
        * scale
    )
    mask = allowed[:, None, None, :]
    masked = jnp.where(mask, scores, NEG)
    top = jnp.max(masked, axis=-1)
    weights = jnp.where(mask, jnp.exp(masked - top[..., None]), 0.0)
    total = jnp.sum(weights, axis=-1)
    summed = jnp.einsum("ihgk,khd->ihgd", weights, value_matrix, precision=lax.Precision.HIGHEST)
    return (top, total, summed)


def join_parts(first, second):
    top = jnp.maximum(first[0], second[0])
    scale_first = jnp.exp(first[0] - top)
    scale_second = jnp.exp(second[0] - top)
    total = first[1] * scale_first + second[1] * scale_second
    summed = first[2] * scale_first[..., None] + second[2] * scale_second[..., None]
    return (top, total, summed)


def plain_local(
    text_states,
    vision_states,
    norm_gain,
    query_weight,
    key_value_weight,
    out_weight,
    query_gain,
    key_norm_gain,
    attn_gate,
    tile_counts,
    tile_mask,
):
    seq_count = lax.axis_size("seq")
    seq_index = lax.axis_index("seq")
    tensor_count = lax.axis_size("tensor")
    tensor_index = lax.axis_index("tensor")
    text_dev = text_states.shape[0]
    text_all = text_dev * seq_count
    vis_dev = vision_states.shape[0]
    head_size = query_gain.shape[0]
    query_local = query_weight.shape[1] // head_size
    normed = root_mean_rows(text_states.astype(jnp.float32), norm_gain.astype(jnp.float32)).astype(
        jnp.bfloat16
    )
    raw_cols, normed_cols = (
        lax.all_to_all(text_states, "seq", split_axis=1, concat_axis=0, tiled=True),
        lax.all_to_all(normed, "seq", split_axis=1, concat_axis=0, tiled=True),
    )
    rows = normed_cols
    query_raw = lax.psum_scatter(
        jnp.dot(rows, query_weight, preferred_element_type=jnp.float32),
        "seq",
        scatter_dimension=0,
        tiled=True,
    )
    query_matrix = root_mean_rows(
        query_raw.reshape(text_dev, query_local, head_size), query_gain
    ).astype(jnp.bfloat16)
    kv_full = jnp.einsum(
        "vd,jdc->jvc",
        vision_states,
        lax.all_gather(key_value_weight, "seq", axis=2, tiled=True),
        preferred_element_type=jnp.float32,
    )
    kv_local = lax.psum_scatter(kv_full, "tensor", scatter_dimension=2, tiled=True)
    kv_heads = kv_local.shape[2] // head_size
    group_size = query_local // kv_heads
    key_matrix = root_mean_rows(
        kv_local[0].reshape(vis_dev, kv_heads, head_size), key_norm_gain
    ).astype(jnp.bfloat16)
    value_matrix = kv_local[1].astype(jnp.bfloat16).reshape(vis_dev, kv_heads, head_size)
    queries_grouped = query_matrix.reshape(text_dev, kv_heads, group_size, head_size)
    query_all = lax.all_gather(queries_grouped, "seq", axis=0, tiled=True)
    allowed = allowed_mask(text_all, seq_index * vis_dev, vis_dev, tile_counts, tile_mask)
    local_parts = partial_attend(query_all, key_matrix, value_matrix.astype(jnp.float32), allowed)
    top, total, summed = combined_all(local_parts, "seq", join_parts)
    attention_all = (
        (summed / total[..., None]).reshape(text_all, query_local * head_size).astype(jnp.bfloat16)
    )
    rows_out = text_all // tensor_count
    rows = attention_all
    branch = lax.psum_scatter(
        jnp.dot(rows, out_weight, preferred_element_type=jnp.float32),
        "tensor",
        scatter_dimension=0,
        tiled=True,
    )
    residual = lax.dynamic_slice_in_dim(raw_cols, tensor_index * rows_out, rows_out, 0)
    return (residual.astype(jnp.float32) + jnp.tanh(attn_gate[0]) * branch).astype(jnp.bfloat16)


MESH = pl.DeviceIdType.MESH
RANKS = 4
CHUNKS = 4
SUBS = 2
SENDS = CHUNKS * SUBS
AHEAD = 3
HEAD = 128
F32, BF16 = jnp.float32, jnp.bfloat16


def landed(ref, sem):
    pltpu.make_async_copy(ref, ref, sem).wait()


def fused_kernel(
    text_ref,
    vision_ref,
    gain_ref,
    qw_hbm,
    kvw_hbm,
    ow_hbm,
    qgain_ref,
    kgain_ref,
    gate_ref,
    counts_ref,
    mask_ref,
    out_ref,
    qw,
    kvw,
    ow,
    near,
    far,
    outer_in,
    active,
    text_out,
    text_in,
    scale_out,
    scale_in,
    query_part,
    query_in,
    mid_out,
    mid_in,
    last_out,
    last_in,
    query_out,
    query_all,
    kv_part,
    kv_in,
    kv_done,
    att_out,
    att_in,
    rows,
    total,
    branch_out,
    branch_in,
    w_sem,
    own_send,
    outer_recv,
    near_recv,
    far_recv,
    cross_send,
    away_send,
    text_send,
    text_recv,
    spread_send,
    scale_send,
    scale_recv,
    qp_send,
    qp_recv,
    mid_sem,
    last_sem,
    qa_send,
    qa_recv,
    kv_send,
    kv_recv,
    done_send,
    done_recv,
    att_send,
    att_recv,
    br_send,
    br_recv,
):
    z = lax.axis_index("seq")
    t = lax.axis_index("tensor")
    core = lax.rem(t, 2)
    inner = (z == 1) | (z == 2)
    away = jnp.where(z < 2, 0, 3)
    toward = jnp.where(z < 2, 1, 2)
    across = 3 - z
    row_chunk = vision_ref.shape[0] // CHUNKS
    sub_rows = row_chunk // SUBS

    def remote(src, dst, send, recv, to_z, to_t):
        return pltpu.make_async_remote_copy(
            src_ref=src,
            dst_ref=dst,
            send_sem=send,
            recv_sem=recv,
            device_id={"seq": to_z, "tensor": to_t},
            device_id_type=MESH,
        )

    loads = [
        pltpu.make_async_copy(src, dst, w_sem.at[i])
        for i, (src, dst) in enumerate(((qw_hbm, qw), (kvw_hbm, kvw), (ow_hbm, ow)))
    ]
    for load in loads:
        load.start()

    barrier = pltpu.get_barrier_semaphore()
    for d in range(1, RANKS * RANKS):
        other = lax.rem(z * RANKS + t + d, RANKS * RANKS)
        pl.semaphore_signal(
            barrier,
            inc=1,
            device_id={"seq": other // RANKS, "tensor": lax.rem(other, RANKS)},
            device_id_type=MESH,
        )

    text = text_ref[...].astype(F32)
    mean_sq = jnp.mean(text * text, axis=-1, keepdims=True)
    scale_out[...] = jnp.broadcast_to(lax.rsqrt(mean_sq + EPS), scale_out.shape)
    part = text.shape[1] // RANKS
    half = part // 2
    piece = half // RANKS
    for b in range(RANKS):
        for p in range(RANKS):
            low, high = b * part + p * piece, b * part + half + p * piece
            text_out[b, p] = jnp.concatenate(
                [text[:, low : low + piece], text[:, high : high + piece]], axis=0
            ).astype(BF16)
    text_in[z] = text_out[z]
    scale_in[z] = scale_out[...]

    pl.semaphore_wait(barrier, RANKS * RANKS - 1)

    def text_copies(d):
        to = lax.rem(z + d, RANKS)
        return (
            remote(scale_out, scale_in.at[z], scale_send.at[d], scale_recv.at[z], to, t),
            remote(
                text_out.at[to, t], text_in.at[z, t], text_send.at[d], text_recv.at[z, t], to, t
            ),
        )

    for d in range(1, RANKS):
        for copy in text_copies(d):
            copy.start()

    def rows_of(u):
        return pl.ds(pl.multiple_of(u * sub_rows, sub_rows), sub_rows)

    def sub(ref, u):
        return ref.at[rows_of(u)]

    def own_outer(u):
        return remote(
            sub(vision_ref, u), sub(outer_in, u), own_send.at[u], outer_recv.at[u], toward, t
        )

    def own_inner(u):
        return remote(sub(vision_ref, u), sub(near, u), own_send.at[u], near_recv.at[u], across, t)

    def cross(u):
        return remote(sub(outer_in, u), sub(far, u), cross_send.at[u], far_recv.at[u], across, t)

    def away_near(u):
        return remote(sub(active, u), sub(near, u), away_send.at[u], near_recv.at[u], away, t)

    def away_far(u):
        return remote(sub(far, u), sub(far, u), away_send.at[SENDS + u], far_recv.at[u], away, t)

    def send_across(m):
        @pl.when(m < SENDS)
        def _():
            own_inner(m).start()

        @pl.when((m >= SENDS) & (m < 2 * SENDS))
        def _():
            u = m - SENDS
            landed(sub(outer_in, u), outer_recv.at[u])
            cross(u).start()

    @pl.when(inner)
    def _():
        for u in range(AHEAD):
            own_inner(u).start()

    @pl.when(~inner)
    def _():
        for u in range(SENDS):
            own_outer(u).start()

    left = mask_ref[0, 0] == 1
    mine = left == (z < 2)

    tile = 512

    def spread_copy(d, e):
        b, to = lax.rem(z + d, RANKS), lax.rem(t + e, RANKS)
        block = text_in.at[b, t]
        return remote(block, block, spread_send.at[d, e], text_recv.at[b, t], z, to)

    def spread_text():
        for d in range(1, RANKS):
            source = lax.rem(z + d, RANKS)
            landed(text_in.at[source, t], text_recv.at[source, t])
            for e in range(1, RANKS):
                spread_copy(d, e).start()

    def whole(b):
        raw = jnp.concatenate([text_in[b, p].astype(F32) for p in range(RANKS)], axis=1)
        return jnp.concatenate([raw[:8], raw[8:]], axis=1)

    def take_text():
        for d in range(1, RANKS):
            source = lax.rem(z + d, RANKS)
            landed(scale_in.at[source], scale_recv.at[source])
            for e in range(1, RANKS):
                p = lax.rem(t + e, RANKS)
                landed(text_in.at[source, p], text_recv.at[source, p])
        gain = gain_ref[pl.ds(pl.multiple_of(z * part, part), part)].astype(F32).reshape(1, part)
        pieces = []
        for b in range(RANKS):
            pieces.append(whole(b) * scale_in[b][:, :1] * gain)
        rows[...] = jnp.concatenate(pieces, axis=0).astype(BF16)
        loads[0].wait()

    def query_tile(n):
        cols = slice(n * tile, (n + 1) * tile)
        got = jnp.dot(rows[...], qw[:, cols], preferred_element_type=F32)
        for b in range(RANKS):
            query_part[b, :, cols] = got[8 * b : 8 * b + 8]

    outer_blocks = (toward, 3 - toward, 3 - z)

    def query_inward(n):
        b = outer_blocks[n]
        return remote(query_part.at[b], query_in.at[b], qp_send.at[n], qp_recv.at[b], toward, t)

    def query_across():
        return remote(mid_out, mid_in, mid_sem.at[0], mid_sem.at[1], across, t)

    def query_outward():
        return remote(last_out, last_in, last_sem.at[0], last_sem.at[1], away, t)

    loads[1].wait()

    def kv_copy(i, d):
        to = lax.rem(t + d, RANKS)
        return remote(kv_part.at[i, to], kv_in.at[i, t], kv_send.at[i, d], kv_recv.at[i, t], z, to)

    def done_copy(i):
        slot = 2 * i + core
        return remote(
            kv_done.at[slot], kv_done.at[slot], done_send.at[i], done_recv.at[i], z, t + 1 - 2 * core
        )

    def finish(i):
        for d in range(1, RANKS):
            source = lax.rem(t + d, RANKS)
            landed(kv_in.at[i, source], kv_recv.at[i, source])
        got = (kv_in[i, 0] + kv_in[i, 1]) + (kv_in[i, 2] + kv_in[i, 3])
        key = root_mean_rows(got[:, :HEAD], kgain_ref[...])
        kv_done[2 * i + core] = jnp.concatenate([key, got[:, HEAD:]], axis=1).astype(BF16)
        done_copy(i).start()

    def multiply(i):
        chunk_rows = active[pl.ds(pl.multiple_of(i * row_chunk, row_chunk), row_chunk), :]
        key = jnp.dot(chunk_rows, kvw[0], preferred_element_type=F32)
        value = jnp.dot(chunk_rows, kvw[1], preferred_element_type=F32)
        half_rows = row_chunk // 2
        for to in range(RANKS):
            r, h = (to % 2) * half_rows, (to // 2) * HEAD
            kv_part[i, to] = jnp.concatenate(
                [key[r : r + half_rows, h : h + HEAD], value[r : r + half_rows, h : h + HEAD]], axis=1
            )
        kv_in[i, t] = kv_part[i, t]
        for d in range(1, RANKS):
            kv_copy(i, d).start()

    @pl.loop(0, CHUNKS)
    def _(c):
        for s in range(SUBS):
            u = c * SUBS + s
            here = rows_of(u)
            landed(sub(near, u), near_recv.at[u])

            @pl.when(inner)
            def _():
                active[here, :] = jnp.where(mine, vision_ref[here, :], near[here, :])
                away_near(u).start()
                send_across(u + AHEAD)

            @pl.when(~inner)
            def _():
                active[here, :] = near[here, :]

        multiply(c)

        @pl.when(c > 0)
        def _():
            finish(c - 1)

        @pl.when(c == 0)
        def _():
            spread_text()

        @pl.when(c == 1)
        def _():
            take_text()
            query_tile(0)
            query_tile(1)

        @pl.when(c == 2)
        def _():
            query_tile(2)
            query_tile(3)

            @pl.when(~inner)
            def _():
                for n in range(3):
                    query_inward(n).start()

        @pl.when((c == 3) & inner)
        def _():
            for b in (z, across, 3 - away):
                landed(query_in.at[b], qp_recv.at[b])
            for n, b in enumerate((across, 3 - away)):
                mid_out[n] = query_part[b] + query_in[b]
            query_across().start()

    heads = part // HEAD

    def take_query(query):
        for side in range(2):
            query_out[side] = jnp.concatenate(
                [
                    root_mean_rows(query[:, h * HEAD : (h + 1) * HEAD], qgain_ref[...])
                    for h in range(side * heads // 2, (side + 1) * heads // 2)
                ],
                axis=0,
            ).astype(BF16)
        for side in range(2):
            start_either(*query_send(side))

    def query_send(side):
        to_t = 2 * side + z // 2
        stays = (t == z) & (t == to_t)
        k = lax.rem(z, 2)
        away_copy = remote(
            query_out.at[side], query_all.at[k], qa_send.at[side], qa_recv.at[k], t, to_t
        )
        here_copy = pltpu.make_async_copy(query_out.at[side], query_all.at[k], qa_recv.at[k])
        return stays, away_copy, here_copy

    def start_either(stays, away_copy, here_copy):
        @pl.when(stays)
        def _():
            here_copy.start()

        @pl.when(~stays)
        def _():
            away_copy.start()

    @pl.loop(CHUNKS, 2 * CHUNKS)
    def _(i):
        for s in range(SUBS):
            u = (i - CHUNKS) * SUBS + s
            here = rows_of(u)
            to = rows_of(u + SENDS)
            landed(sub(far, u), far_recv.at[u])

            @pl.when(inner)
            def _():
                away_far(u).start()
                send_across(u + SENDS + AHEAD)
                active[to, :] = jnp.where(mine, outer_in[here, :], far[here, :])

            @pl.when(~inner)
            def _():
                active[to, :] = jnp.where(mine, vision_ref[here, :], far[here, :])

        multiply(i)
        finish(i - 1)

        @pl.when((i == CHUNKS + 1) & inner)
        def _():
            landed(mid_in, mid_sem.at[1])
            last_out[...] = query_part[away] + mid_in[1]
            query_outward().start()
            take_query((query_part[z] + query_in[z]) + mid_in[0])

        @pl.when((i == CHUNKS + 2) & ~inner)
        def _():
            landed(last_in, last_sem.at[1])
            take_query(query_part[z] + last_in[...])

    finish(2 * CHUNKS - 1)
    for k in range(2):
        landed(query_all.at[k], qa_recv.at[k])
    for i in range(2 * CHUNKS):
        slot = 2 * i + 1 - core
        landed(kv_done.at[slot], done_recv.at[i])
    slots = 2 * vision_ref.shape[0]
    both = kv_done[...].reshape(slots, 2 * HEAD)
    queries = query_all[...].reshape(2 * query_all.shape[1], HEAD)
    scores = lax.dot_general(
        queries, both[:, :HEAD], (((1,), (1,)), ((), ())), preferred_element_type=F32
    ) * (HEAD**-0.5)
    place = lax.broadcasted_iota(jnp.int32, scores.shape, 1)
    swapped = jnp.where(place < slots // 2, place + slots // 2, place - slots // 2)
    place = jnp.where(left, swapped, place)
    valid = place < jnp.where(left, counts_ref[0], counts_ref[1])
    scores = jnp.where(valid, scores, NEG)
    top = jnp.max(scores, axis=-1, keepdims=True)
    weights = jnp.where(valid, jnp.exp(scores - top), 0.0)
    norm = jnp.sum(weights, axis=-1, keepdims=True)
    high = weights.astype(BF16)
    low = (weights - high.astype(F32)).astype(BF16)
    value = both[:, HEAD:]
    summed = jnp.dot(high, value, preferred_element_type=F32) + jnp.dot(
        low, value, preferred_element_type=F32
    )
    att_out[...] = (summed / norm).astype(BF16)

    def att_copy(d):
        to_z = lax.rem(z + d, RANKS)
        stays = (to_z == z) & (t == z)
        return (
            stays,
            remote(att_out, att_in.at[t], att_send.at[d], att_recv.at[t], to_z, z),
            pltpu.make_async_copy(att_out, att_in.at[t], att_recv.at[t]),
        )

    for d in (2, 1, 3):
        stays, away_copy, here_copy = att_copy(d)
        away_copy.start()
    start_either(*att_copy(0))
    loads[2].wait()
    for source in range(RANKS):
        landed(att_in.at[source], att_recv.at[source])
    arrived = [att_in[source].astype(F32) for source in range(RANKS)]
    group = 8
    for side in range(2):
        for j in range(group):
            column = (side * group + j) * HEAD
            rows[:, column : column + HEAD] = jnp.concatenate(
                [
                    arrived[2 * side + b // 2][(b % 2) * 64 + j * 8 : (b % 2) * 64 + j * 8 + 8]
                    for b in range(RANKS)
                ],
                axis=0,
            ).astype(BF16)

    def branch_copy(n, d):
        to = lax.rem(t + d, RANKS)
        return remote(
            branch_out.at[n, to], branch_in.at[n, t], br_send.at[n, d], br_recv.at[n, t], z, to
        )

    for n in range(2):
        parts = []
        for s in range(2):
            start = s * half + n * tile
            got = jnp.dot(rows[...], ow[:, start : start + tile], preferred_element_type=F32)
            total[:, start : start + tile] = got
            parts.append(got)
        for to in range(RANKS):
            branch_out[n, to] = jnp.concatenate(
                [got[8 * to : 8 * to + 8] for got in parts], axis=0
            ).astype(BF16)
        for d in (2, 1, 3):
            branch_copy(n, d).start()

    gate = jnp.tanh(jnp.full((8, tile), gate_ref[0], F32))
    residual = whole(t)
    own_rows = pl.ds(pl.multiple_of(8 * t, 8), 8)
    for n in range(2):
        for d in range(1, RANKS):
            source = lax.rem(t + d, RANKS)
            landed(branch_in.at[n, source], br_recv.at[n, source])
        others = []
        for d in range(1, RANKS):
            others.append(branch_in[n, lax.rem(t + d, RANKS)].astype(F32))
        other = (others[0] + others[1]) + others[2]
        for s in range(2):
            start = s * half + n * tile
            branch = total[own_rows, start : start + tile] + other[8 * s : 8 * s + 8]
            base = residual[:, start : start + tile]
            out_ref[:, start : start + tile] = (base + gate * branch).astype(BF16)

    for d in range(1, RANKS):
        for copy in text_copies(d):
            copy.wait_send()
        for e in range(1, RANKS):
            spread_copy(d, e).wait_send()
        att_copy(d)[1].wait_send()
        for n in range(2):
            branch_copy(n, d).wait_send()
    stays, away_copy, here_copy = att_copy(0)

    @pl.when(~stays)
    def _():
        away_copy.wait_send()

    for side in range(2):
        q_stays, q_away, q_here = query_send(side)

        @pl.when(~q_stays)
        def _():
            q_away.wait_send()

    @pl.when(inner)
    def _():
        query_across().wait_send()
        query_outward().wait_send()

    @pl.when(~inner)
    def _():
        for n in range(3):
            query_inward(n).wait_send()

    @pl.loop(0, SENDS)
    def _(u):
        own_inner(u).wait_send()

        @pl.when(inner)
        def _():
            cross(u).wait_send()
            away_near(u).wait_send()
            away_far(u).wait_send()

    @pl.loop(0, 2 * CHUNKS)
    def _(i):
        for d in range(1, RANKS):
            kv_copy(i, d).wait_send()
        done_copy(i).wait_send()


def fused_fits(text_states, vision_states, query_weight, key_value_weight, out_weight, query_gain, tile_counts, tile_mask):
    return (
        lax.axis_size("seq") == RANKS
        and lax.axis_size("tensor") == RANKS
        and tile_mask.shape == (1, 2)
        and tile_counts.shape == (2,)
        and text_states.shape == (8, 8192)
        and vision_states.shape == (256, 2048)
        and query_weight.shape == (2048, 2048)
        and out_weight.shape == (2048, 2048)
        and key_value_weight.shape == (2, 2048, 256)
        and query_gain.shape == (HEAD,)
    )


def fused_local(
    text_states,
    vision_states,
    norm_gain,
    query_weight,
    key_value_weight,
    out_weight,
    query_gain,
    key_norm_gain,
    attn_gate,
    tile_counts,
    tile_mask,
):
    part = query_weight.shape[0]
    tokens, slots = text_states.shape[0], vision_states.shape[0]
    chunk = slots // CHUNKS
    vmem = pl.BlockSpec(memory_space=pltpu.VMEM)
    smem = pl.BlockSpec(memory_space=pltpu.SMEM)
    hbm = pl.BlockSpec(memory_space=pl.ANY)
    block = pltpu.VMEM((slots, part), BF16)
    dma = pltpu.SemaphoreType.DMA
    return pl.pallas_call(
        fused_kernel,
        out_shape=jax.ShapeDtypeStruct((tokens, part), BF16),
        in_specs=[vmem, vmem, vmem, hbm, hbm, hbm, vmem, vmem, smem, smem, smem],
        out_specs=vmem,
        scratch_shapes=[
            pltpu.VMEM(query_weight.shape, BF16),
            pltpu.VMEM(key_value_weight.shape, BF16),
            pltpu.VMEM(out_weight.shape, BF16),
            block,
            block,
            block,
            pltpu.VMEM((2 * slots, part), BF16),
            pltpu.VMEM((RANKS, RANKS, 16, part // 8), BF16),
            pltpu.VMEM((RANKS, RANKS, 16, part // 8), BF16),
            pltpu.VMEM((8, HEAD), F32),
            pltpu.VMEM((RANKS, 8, HEAD), F32),
            pltpu.VMEM((RANKS, 8, part), F32),
            pltpu.VMEM((RANKS, 8, part), F32),
            pltpu.VMEM((2, 8, part), F32),
            pltpu.VMEM((2, 8, part), F32),
            pltpu.VMEM((8, part), F32),
            pltpu.VMEM((8, part), F32),
            pltpu.VMEM((2, 64, HEAD), BF16),
            pltpu.VMEM((2, 64, HEAD), BF16),
            pltpu.VMEM((2 * CHUNKS, RANKS, chunk // 2, 2 * HEAD), F32),
            pltpu.VMEM((2 * CHUNKS, RANKS, chunk // 2, 2 * HEAD), F32),
            pltpu.VMEM((4 * CHUNKS, chunk // 2, 2 * HEAD), BF16),
            pltpu.VMEM((128, HEAD), BF16),
            pltpu.VMEM((RANKS, 128, HEAD), BF16),
            pltpu.VMEM((32, part), BF16),
            pltpu.VMEM((32, part), F32),
            pltpu.VMEM((2, RANKS, 16, 512), BF16),
            pltpu.VMEM((2, RANKS, 16, 512), BF16),
            dma((3,)),
            dma((SENDS,)),
            dma((SENDS,)),
            dma((SENDS,)),
            dma((SENDS,)),
            dma((SENDS,)),
            dma((2 * SENDS,)),
            dma((RANKS,)),
            dma((RANKS, RANKS)),
            dma((RANKS, RANKS)),
            dma((RANKS,)),
            dma((RANKS,)),
            dma((RANKS,)),
            dma((RANKS,)),
            dma((2,)),
            dma((2,)),
            dma((2,)),
            dma((2,)),
            dma((2 * CHUNKS, RANKS)),
            dma((2 * CHUNKS, RANKS)),
            dma((2 * CHUNKS,)),
            dma((2 * CHUNKS,)),
            dma((RANKS,)),
            dma((RANKS,)),
            dma((2, RANKS)),
            dma((2, RANKS)),
        ],
        compiler_params=pltpu.CompilerParams(
            collective_id=0, has_side_effects=True, vmem_limit_bytes=56 * 1024 * 1024
        ),
    )(
        text_states,
        vision_states,
        norm_gain,
        query_weight,
        key_value_weight,
        out_weight,
        query_gain.reshape(1, HEAD),
        key_norm_gain.reshape(1, HEAD),
        attn_gate,
        tile_counts,
        tile_mask,
    )


def local(*args):
    text, vision, _, query_weight, kv_weight, out_weight, query_gain, _, _, counts, mask = args
    if fused_fits(text, vision, query_weight, kv_weight, out_weight, query_gain, counts, mask):
        return fused_local(*args)
    return plain_local(*args)


def solution(mesh):
    return jax.shard_map(
        local,
        mesh=mesh,
        in_specs=(
            P(("groups", "seq"), None),
            P(("groups", "seq"), "tensor"),
            P(),
            P("seq", "tensor"),
            P(None, "tensor", "seq"),
            P("tensor", "seq"),
            P(),
            P(),
            P(),
            P("groups"),
            P("groups", None),
        ),
        out_specs=P(("groups", "tensor"), "seq"),
        check_vma=False,
    )
```
